32 devices in a mesh: hi: 4 (over x, core), lo: 8 (over z, y).
Axes of the slice: x: 2, y: 2, z: 4, core: 2. Of those that a mesh axis runs over, the one named last changes fastest.
Arguments:
- design: float32 [65536, 512], P(('hi', 'lo')), may hold values from -40 to 40
- signs: int32 [65536], P(('hi', 'lo')), may hold values from 0 to 1
- samples: int32 [4096], P(('hi', 'lo')), may hold values from 0 to 65535, as said below
Outputs:
- sketch: float32 [4096, 512], P(('hi', 'lo'))
- gram: float32 [512, 512], P(('hi', 'lo'))
The draws below stay inside these ranges and needn't reach their ends.
Inputs may be any that keep to these rules, and one draw needn't show every extreme that they name: `samples`: row indices into the whole design. Among the 128 entries owned by one device, at most 8 fall in the rows of any one device (rows p * 2048 to (p + 1) * 2048 - 1 for device p, devices in hi+lo order), and in every draw one device supplies exactly 8 to every owner. Likewise, among one owner's entries at most 8 have a local row (index modulo 2048) in any one range s * 64 to (s + 1) * 64 - 1, and for every owner one such range holds exactly 8.
All inputs are finite; a program needn't handle non-finite values.
Results may differ from the reference program's by a relative error of at most 0.00011.
Values sent between devices are 32-bit elements; how exact they have to be, the bound alone decides.
No kernel may reach another device: no remote copies, remote signals or barrier semaphores. Data moves between devices by JAX's collectives and lax.ppermute only.
A program may use at most 64 MiB of HBM per device.

```python
import math
import jax
import jax.numpy as jnp
from jax import lax

COLS = 512
ROWS_DEV = 2048
SAMP_DEV = 128
N_ROWS = 65536
DEVICES = 32


def draw_design(key, part):
    key = jax.random.fold_in(key, 7)
    total = ROWS_DEV * DEVICES
    keys = jax.random.split(key, 3)
    col_scale = jnp.exp(jax.random.uniform(keys[0], (COLS,), jnp.float32, math.log(0.3), math.log(3.0)))
    row_scale = jnp.exp(jax.random.uniform(keys[1], (total, 1), jnp.float32, math.log(0.3), math.log(3.0)))
    base = jnp.clip(jax.random.normal(keys[2], (total, COLS), jnp.float32), -4.0, 4.0)
    return jnp.clip(base * row_scale * col_scale[None, :], -40.0, 40.0)


def draw_samples(key, part):
    key = jax.random.fold_in(key, 11)
    keys = jax.random.split(key, 6)
    owners = DEVICES
    capacity = max(2, 2 * SAMP_DEV // DEVICES)
    slice_len = ROWS_DEV // DEVICES
    heat = jax.random.randint(keys[0], (owners,), 0, 4)
    hottest = jax.random.randint(keys[1], (), 0, owners)
    heat = jnp.where(jnp.arange(owners) == hottest, 5, heat)
    slot_count = owners * capacity
    slot_source = jnp.arange(slot_count, dtype=jnp.int32) // capacity
    noise = jax.random.randint(keys[2], (owners, slot_count), 0, 4096)
    score = (heat[slot_source][None, :] * 4096 + noise) * 16384 + jnp.arange(slot_count, dtype=jnp.int32)[None, :]
    chosen = jax.lax.top_k(score, SAMP_DEV)[1]
    source = chosen // capacity
    hot_slice = jax.random.randint(keys[4], (owners, 1), 0, owners)
    slice_noise = jax.random.randint(keys[5], (owners, slot_count), 0, 4096)
    boost = jnp.where(slot_source[None, :] == hot_slice, 4096, 0)
    slice_score = (slice_noise + boost) * 16384 + jnp.arange(slot_count, dtype=jnp.int32)[None, :]
    slice_pick = jax.lax.top_k(slice_score, SAMP_DEV)[1] // capacity
    offsets = jax.random.randint(keys[3], (owners, SAMP_DEV), 0, slice_len)
    local_rows = slice_pick * slice_len + offsets
    return (source * ROWS_DEV + local_rows).reshape(owners * SAMP_DEV).astype(jnp.int32)


def plant(entries, stream_key, least, largest):
    longest = entries.shape.index(max(entries.shape))
    spots = []
    for shift in (0, 1):
        where = [jax.random.randint(jax.random.fold_in(stream_key, axis), (), 0, length) for axis, length in enumerate(entries.shape)]
        where[longest] = (where[longest] + shift) % entries.shape[longest]
        spots.append(tuple(where))
    return entries.at[spots[0]].set(least).at[spots[1]].set(largest)


def setup_inputs(seed: int = 0) -> dict:
    key_list = jax.random.split(jax.random.key(seed), 4)
    design = draw_design(jax.random.fold_in(key_list[3], 71), 0)
    signs = plant(jax.random.randint(key_list[1], (N_ROWS,), 0, 2), jax.random.fold_in(key_list[1], 1), 0, 1).astype(jnp.int32)
    samples = draw_samples(jax.random.fold_in(key_list[3], 71), 0)
    return dict(design=design, signs=signs, samples=samples)


def reference(design, signs, samples):
    total = design.shape[0]
    width = design.shape[1]
    flipped = design * (2 * signs - 1).astype(design.dtype)[:, None]
    levels = total.bit_length() - 1
    for level in range(levels):
        half = 2 ** level
        shaped = flipped.reshape(total // (2 * half), 2, half, width)
        upper = shaped[:, 0]
        lower = shaped[:, 1]
        flipped = jnp.stack([upper + lower, upper - lower], axis=1).reshape(total, width)
    mixed = flipped / math.sqrt(total)
    sketch = mixed[samples]
    gram = jnp.dot(sketch.T, sketch, precision=lax.Precision.HIGHEST, preferred_element_type=jnp.float32) / samples.shape[0]
    return (sketch, gram)
```

```python
import functools
import math

import jax
import jax.numpy as jnp
from jax import lax
from jax.experimental import pallas as pl
from jax.experimental.pallas import tpu as pltpu
from jax.sharding import Mesh, PartitionSpec as P

VMEM = pl.BlockSpec(memory_space=pltpu.VMEM)
SMEM = pl.BlockSpec(memory_space=pltpu.SMEM)
LIMIT = pltpu.CompilerParams(vmem_limit_bytes=48 * 1024 * 1024)
BLOCK = 256
LANES = 128


def walsh(values):
    half = 1
    while half < len(values):
        out = list(values)
        for i in range(len(values)):
            if not i & half:
                out[i] = values[i] + values[i | half]
                out[i | half] = values[i] - values[i | half]
        values = out
        half *= 2
    return values


def transform_kernel(own_ref, oth_ref, own_sign_ref, oth_sign_ref, mixed_ref, part_ref):
    rows, cols = own_ref.shape
    blocks, tiles = rows // BLOCK, cols // LANES
    common = lax.broadcasted_iota(jnp.int32, (BLOCK, BLOCK), 0) & lax.broadcasted_iota(
        jnp.int32, (BLOCK, BLOCK), 1
    )
    for shift in (4, 2, 1):
        common = common ^ (common >> shift)
    had = (1 - 2 * (common & 1)).astype(jnp.float32)

    for which, (ref, sign_ref) in enumerate(((own_ref, own_sign_ref), (oth_ref, oth_sign_ref))):

        def one_block(b, carry, ref=ref, sign_ref=sign_ref, which=which):
            left = (had * sign_ref[pl.ds(b, 1), :]).astype(jnp.bfloat16)
            full = ref[pl.ds(pl.multiple_of(b * BLOCK, BLOCK), BLOCK), :]
            high = full.astype(jnp.bfloat16)
            low = (full - high.astype(jnp.float32)).astype(jnp.bfloat16)
            part_ref[which, b] = jnp.dot(
                left, high, preferred_element_type=jnp.float32
            ) + jnp.dot(left, low, preferred_element_type=jnp.float32)
            return carry

        lax.fori_loop(0, blocks, one_block, 0)

    def one_chunk(chunk, carry):
        start = pl.multiple_of(chunk * 8, 8)
        for tile in range(tiles):
            lanes = slice(tile * LANES, (tile + 1) * LANES)
            own = walsh([part_ref[0, b, pl.ds(start, 8), lanes] for b in range(blocks)])
            oth = walsh([part_ref[1, b, pl.ds(start, 8), lanes] for b in range(blocks)])
            for b in range(blocks):
                both = (own[b] + oth[b], own[b] - oth[b])
                for core in range(2):
                    for negative in range(2):
                        row = (negative * 2 + core) * rows + b * BLOCK + start
                        mixed_ref[pl.ds(row * tiles + tile, 8, stride=tiles), :] = (
                            -both[core] if negative else both[core]
                        )
        return carry

    lax.fori_loop(0, BLOCK // 8, one_chunk, 0)


def transform(own, oth, own_sign, oth_sign):
    rows, cols = own.shape
    return pl.pallas_call(
        transform_kernel,
        out_shape=jax.ShapeDtypeStruct((4 * rows * cols // LANES, LANES), jnp.float32),
        in_specs=[VMEM] * 4,
        out_specs=VMEM,
        scratch_shapes=[pltpu.VMEM((2, rows // BLOCK, BLOCK, cols), jnp.float32)],
        compiler_params=LIMIT,
        cost_estimate=pl.CostEstimate(
            flops=4 * rows * BLOCK * cols * 2, bytes_accessed=6 * rows * cols * 4, transcendentals=0
        ),
    )(own, oth, own_sign, oth_sign)


def gather_kernel(plans, tiles, code_ref, mixed_ref, *out_refs):
    for out_ref, (starts, count) in zip(out_refs, plans):
        for place, start in enumerate(starts):

            def one(i, carry, out_ref=out_ref, place=place, start=start, count=count):
                code = code_ref[start + i]
                out_ref[pl.ds((place * count + i) * tiles, tiles), :] = mixed_ref[
                    pl.ds(pl.multiple_of(code * tiles, tiles), tiles), :
                ]
                return carry

            lax.fori_loop(0, count, one, 0, unroll=4)


def gather(plans, tiles, code, mixed):
    total = sum(len(starts) * count for starts, count in plans)
    return pl.pallas_call(
        functools.partial(gather_kernel, plans, tiles),
        out_shape=[
            jax.ShapeDtypeStruct((len(starts) * count * tiles, LANES), jnp.float32)
            for starts, count in plans
        ],
        in_specs=[SMEM, VMEM],
        out_specs=[VMEM] * len(plans),
        compiler_params=LIMIT,
        cost_estimate=pl.CostEstimate(
            flops=0, bytes_accessed=8 * total * tiles * LANES, transcendentals=0
        ),
    )(code, mixed)


def gram_kernel(scale, inverse_total, core_ref, own_ref, oth_ref, sketch_ref, gram_ref, both_ref):
    samp, cols = sketch_ref.shape
    tiles = cols // LANES
    for tile in range(tiles):
        lanes = slice(tile * LANES, (tile + 1) * LANES)
        mine = own_ref[pl.ds(tile, samp, stride=tiles), :] * scale
        sketch_ref[:, lanes] = mine
        both_ref[:samp, lanes] = mine
        both_ref[samp:, lanes] = oth_ref[pl.ds(tile, samp, stride=tiles), :] * scale
    rows = gram_ref.shape[0]
    width = cols * rows // cols // 2
    for upper in range(2):
        start = pl.multiple_of(upper * (cols // 2) + core_ref[0] * width, LANES)
        gram_ref[upper * width : (upper + 1) * width, :] = (
            lax.dot_general(
                both_ref[:, pl.ds(start, width)],
                both_ref[...],
                (((0,), (0,)), ((), ())),
                precision=lax.Precision.HIGHEST,
                preferred_element_type=jnp.float32,
            )
            * inverse_total
        )


def swap(block, bit):
    return lax.ppermute(block, bit, [(0, 1), (1, 0)])


def per_device(bits, design, signs, samples):
    rows, cols = design.shape
    samp = samples.shape[0]
    tiles = cols // LANES
    devices = 2 ** len(bits)
    high, core, low = bits[0], bits[1], bits[:1:-1]
    steps = [high, *low]
    own_index = lax.axis_index(tuple(bits))
    core_bit = len(low)

    oth_design = swap(design, core)
    oth_signs = swap(signs, core)
    listed = samples
    for bit in steps:
        listed = jnp.concatenate([listed, swap(listed, bit)])

    sign_rows = [(2 * s - 1).astype(jnp.float32).reshape(rows // BLOCK, BLOCK) for s in (signs, oth_signs)]
    mixed = transform(design, oth_design, *sign_rows)

    source = listed // rows
    parity = source & own_index
    shift = 1
    while shift < devices:
        parity = parity ^ (parity >> shift)
        shift *= 2
    code = ((parity & 1) * 2 + (source >> core_bit & 1)) * rows + listed % rows

    third = (samp // 3 + 2) // 2 * 2
    counts = [third, third, samp - 2 * third]
    owners = devices // 2
    orders = []
    for part in range(3):
        order = [(part + i) % 3 for i in range(3)]
        orders.append(order + list(range(3, len(steps))))

    def starts(part, first):
        order = orders[part]
        found = []
        for place in range(owners // 2):
            owner = first << order[0]
            for level, bit in enumerate(order[1:]):
                owner |= (place >> (len(order) - 2 - level) & 1) << bit
            found.append(owner * samp + sum(counts[:part]))
        return found, counts[part]

    sent = [gather([starts(part, 1)], tiles, code, mixed)[0] for part in range(3)]
    arrived = [swap(sent[part], steps[part]) for part in range(3)]
    held = gather([starts(part, 0) for part in range(3)], tiles, code, mixed)
    for level in range(1, 3):
        sends, keeps = [], []
        for part in range(3):
            half = held[part].shape[0] // 2
            keeps.append(held[part][:half] + arrived[part][:half])
            sends.append(held[part][half:] + arrived[part][half:])
        arrived = [swap(sends[part], steps[orders[part][level]]) for part in range(3)]
        held = keeps
    pieces = [held[part] + arrived[part] for part in range(3)]
    pieces = [p.reshape(-1, counts[i] * tiles, LANES) for i, p in enumerate(pieces)]
    whole = jnp.concatenate(pieces, axis=1)
    for level in range(3, len(steps)):
        half = whole.shape[0] // 2
        whole = whole[:half] + swap(whole[half:], steps[level])
    own_sum = whole[0]
    oth_sum = swap(own_sum, core)

    half_rows = cols // 2
    sketch, product = pl.pallas_call(
        functools.partial(gram_kernel, 1.0 / math.sqrt(rows * devices), 1.0 / (samp * devices)),
        out_shape=[
            jax.ShapeDtypeStruct((samp, cols), jnp.float32),
            jax.ShapeDtypeStruct((half_rows, cols), jnp.float32),
        ],
        in_specs=[SMEM, VMEM, VMEM],
        out_specs=[VMEM, VMEM],
        scratch_shapes=[pltpu.VMEM((2 * samp, cols), jnp.float32)],
        compiler_params=LIMIT,
    )(lax.axis_index(core).astype(jnp.int32).reshape(1), own_sum, oth_sum)

    gathered = lax.all_to_all(product, (high, *reversed(low)), split_axis=0, concat_axis=0, tiled=True)
    gram = jnp.sum(gathered.reshape(owners, cols // devices, cols), axis=0)
    return sketch, gram


def solution(mesh):
    width = [size.bit_length() - 1 for size in mesh.devices.shape]
    bits = [f"{axis}{i}" for axis, w in zip(mesh.axis_names, width) for i in reversed(range(w))]
    split = Mesh(mesh.devices.reshape((2,) * len(bits)), tuple(bits))
    every = tuple(bits)
    return jax.shard_map(
        functools.partial(per_device, bits),
        mesh=split,
        in_specs=(P(every, None), P(every), P(every)),
        out_specs=(P(every, None), P(every, None)),
        check_vma=False,
    )
```

```python
import functools
import math

import jax
import jax.numpy as jnp
from jax import lax
from jax.experimental import pallas as pl
from jax.experimental.pallas import tpu as pltpu
from jax.sharding import Mesh, PartitionSpec as P

HBM = pl.BlockSpec(memory_space=pltpu.HBM)
VMEM = pl.BlockSpec(memory_space=pltpu.VMEM)
SMEM = pl.BlockSpec(memory_space=pltpu.SMEM)
BLOCK = 256
LANES = 128
BATCH = 16
GROUPS = 1
NEGATIVE = 1 << 30


def limit(mib):
    return pltpu.CompilerParams(vmem_limit_bytes=mib * 1024 * 1024)


def cost(flops, moved):
    return pl.CostEstimate(flops=flops, bytes_accessed=moved, transcendentals=0)


def walsh(values):
    half = 1
    while half < len(values):
        out = list(values)
        for i in range(len(values)):
            if not i & half:
                out[i] = values[i] + values[i | half]
                out[i | half] = values[i] - values[i | half]
        values = out
        half *= 2
    return values


def transform_kernel(own_ref, oth_ref, own_sign_ref, oth_sign_ref, table_ref, held_ref, part_ref, sems):
    blocks, cols = part_ref.shape[1], part_ref.shape[3]
    tiles = cols // LANES
    copies = [
        pltpu.make_async_copy(
            ref.at[pl.ds(b * BLOCK, BLOCK)], held_ref.at[core, b], sems.at[core, b]
        )
        for core, ref in enumerate((own_ref, oth_ref))
        for b in range(blocks)
    ]
    for copy in copies:
        copy.start()
    common = lax.broadcasted_iota(jnp.int32, (BLOCK, BLOCK), 0) & lax.broadcasted_iota(
        jnp.int32, (BLOCK, BLOCK), 1
    )
    for shift in (4, 2, 1):
        common = common ^ (common >> shift)
    had = (1 - 2 * (common & 1)).astype(jnp.float32)
    for core, sign_ref in enumerate((own_sign_ref, oth_sign_ref)):
        for b in range(blocks):
            copies[core * blocks + b].wait()
            left = (had * sign_ref[b : b + 1, :]).astype(jnp.bfloat16)
            full = held_ref[core, b]
            high = full.astype(jnp.bfloat16)
            low = (full - high.astype(jnp.float32)).astype(jnp.bfloat16)
            part_ref[core, b] = jnp.dot(
                jnp.concatenate([left, left], axis=1),
                jnp.concatenate([high, low], axis=0),
                preferred_element_type=jnp.float32,
            )

    def one_chunk(chunk, carry):
        start = pl.multiple_of(chunk * 8, 8)
        for tile in range(tiles):
            lanes = slice(tile * LANES, (tile + 1) * LANES)
            own = walsh([part_ref[0, b, pl.ds(start, 8), lanes] for b in range(blocks)])
            oth = walsh([part_ref[1, b, pl.ds(start, 8), lanes] for b in range(blocks)])
            for b in range(blocks):
                for core, value in enumerate((own[b] + oth[b], own[b] - oth[b])):
                    row = (core * blocks + b) * BLOCK + start
                    table_ref[pl.ds(row * tiles + tile, 8, stride=tiles), :] = value
        return carry

    lax.fori_loop(0, BLOCK // 8, one_chunk, 0)


def transform(own, oth, own_sign, oth_sign):
    count, cols = own.shape
    blocks = count // BLOCK
    return pl.pallas_call(
        transform_kernel,
        out_shape=jax.ShapeDtypeStruct((2 * count * cols // LANES, LANES), jnp.float32),
        in_specs=[HBM, HBM, VMEM, VMEM],
        out_specs=VMEM,
        scratch_shapes=[
            pltpu.VMEM((2, blocks, BLOCK, cols), jnp.float32),
            pltpu.VMEM((2, blocks, BLOCK, cols), jnp.float32),
            pltpu.SemaphoreType.DMA((2, blocks)),
        ],
        compiler_params=limit(20),
        cost_estimate=cost(8 * count * BLOCK * cols, 16 * count * cols),
    )(own, oth, own_sign, oth_sign)


def gather_kernel(plans, tiles, code_ref, table_ref, *out_refs):
    for out_ref, (starts, count) in zip(out_refs, plans):

        def copy(first, base, number, out_ref=out_ref):
            rows = []
            for i in range(number):
                code = code_ref[first + i]
                at = pl.multiple_of(code & (NEGATIVE - 1), tiles)
                row = table_ref[pl.ds(at, tiles), :]
                rows.append(jnp.where(code >= NEGATIVE, -row, row))
            for i, row in enumerate(rows):
                out_ref[pl.ds(pl.multiple_of((base + i) * tiles, tiles), tiles), :] = row

        for place, start in enumerate(starts):
            whole = count // BATCH

            def batch(step, carry, start=start, place=place, count=count, copy=copy):
                copy(start + step * BATCH, place * count + step * BATCH, BATCH)
                return carry

            lax.fori_loop(0, whole, batch, 0)
            if count % BATCH:
                copy(start + whole * BATCH, place * count + whole * BATCH, count % BATCH)


def gather(plans, tiles, code, table):
    total = sum(len(starts) * count for starts, count in plans)
    return pl.pallas_call(
        functools.partial(gather_kernel, plans, tiles),
        out_shape=[
            jax.ShapeDtypeStruct((len(starts) * count * tiles, LANES), jnp.float32)
            for starts, count in plans
        ],
        in_specs=[SMEM, VMEM],
        out_specs=[VMEM] * len(plans),
        compiler_params=limit(4),
        cost_estimate=cost(0, 8 * total * tiles * LANES),
    )(code, table)


def gram_kernel(scale, inverse_total, core_ref, *refs):
    sums, (sketch_ref, gram_ref, both_ref) = refs[:-3], refs[-3:]
    samp, cols = sketch_ref.shape
    tiles = cols // LANES
    for tile in range(tiles):
        lanes = slice(tile * LANES, (tile + 1) * LANES)
        at = 0
        for ref in sums:
            count = ref.shape[0] // tiles
            both_ref[at : at + count, lanes] = ref[pl.ds(tile, count, stride=tiles), :] * scale
            at += count
    sketch_ref[...] = both_ref[:samp, :]
    width = gram_ref.shape[0] // 2
    for upper in range(2):
        start = pl.multiple_of(upper * (cols // 2) + core_ref[0] * width, LANES)
        gram_ref[upper * width : (upper + 1) * width, :] = (
            lax.dot_general(
                both_ref[:, pl.ds(start, width)],
                both_ref[...],
                (((0,), (0,)), ((), ())),
                precision=lax.Precision.HIGHEST,
                preferred_element_type=jnp.float32,
            )
            * inverse_total
        )


def swap(block, bit):
    return lax.ppermute(block, bit, [(0, 1), (1, 0)])


def exclusive(block, place, axis):
    while block.shape[axis] > 1:
        half = block.shape[axis] // 2
        upper = lax.slice_in_dim(block, half, 2 * half, axis=axis)
        lower = lax.slice_in_dim(block, 0, half, axis=axis)
        block = jnp.where(place & half == half, upper, lower)
    return jnp.squeeze(block, axis)


def reduce_pairs(block, axes):
    own = lax.axis_index(axes)
    total = exclusive(block, own, 0)
    for flip in (3, 2, 1):
        route = [(i, i ^ flip) for i in range(4)]
        total += lax.ppermute(exclusive(block, own ^ flip, 0), axes, route)
    return total


def reduce_gram(block, high, low):
    first, rest = low[0], low[1:]
    block = block.reshape(2, -1, 2, *block.shape[2:])
    block = jnp.moveaxis(block, 2, 1).reshape(4, -1, *block.shape[3:])
    block = reduce_pairs(block, (high, first))
    while rest:
        if len(rest) >= 2:
            block = reduce_pairs(block.reshape(4, -1, *block.shape[1:]), (rest[-1], rest[-2]))
            rest = rest[:-2]
        else:
            last = rest[-1]
            own = lax.axis_index(last)
            block = block.reshape(2, -1, *block.shape[1:])
            block = exclusive(block, own, 0) + swap(exclusive(block, 1 - own, 0), last)
            rest = rest[:-1]
    return block[0]


def per_device(bits, design, signs, samples):
    rows, cols = design.shape
    samp = samples.shape[0]
    tiles = cols // LANES
    devices = 2 ** len(bits)
    high, core, low = bits[0], bits[1], bits[:1:-1]
    steps = [high, *low]
    own_index = lax.axis_index(tuple(bits))
    core_bit = len(low)

    oth_design = swap(design, core)
    oth_signs = swap(signs, core)
    sign_rows = [(2 * s - 1).astype(jnp.float32).reshape(rows // BLOCK, BLOCK) for s in (signs, oth_signs)]
    listed = lax.optimization_barrier(samples ^ (own_index >> len(bits)))
    for bit in steps[:-1]:
        listed = jnp.concatenate([listed, swap(listed, bit)])
    listed, oth_design = lax.optimization_barrier((listed, oth_design))
    listed = jnp.concatenate([listed, swap(listed, steps[-1])])
    mixed = transform(design, oth_design, *sign_rows)

    source = listed // rows
    parity = source & own_index
    shift = 1
    while shift < devices:
        parity = parity ^ (parity >> shift)
        shift *= 2
    code = ((source >> core_bit & 1) * rows + listed % rows) * tiles + (parity & 1) * NEGATIVE

    owners = devices // 2
    groups = GROUPS
    group_samp = samp // groups
    third = (group_samp // 3 + 2) // 2 * 2
    counts = [third, third, group_samp - 2 * third] * groups
    orders = []
    for part in range(3):
        order = [(part + i) % 3 for i in range(3)]
        orders.append(order + list(range(3, len(steps))))

    def plan(piece, first):
        order = orders[piece % 3]
        found = []
        for place in range(owners // 2):
            owner = first << order[0]
            for level, bit in enumerate(order[1:]):
                owner |= (place >> (len(order) - 2 - level) & 1) << bit
            found.append(owner * samp + sum(counts[:piece]))
        return found, counts[piece]

    arrived, held = [], []
    for piece in range(3 * groups):
        sent = gather([plan(piece, 1)], tiles, code, mixed)[0]
        arrived.append(swap(sent, steps[piece % 3]))
    for group in range(groups):
        held += gather([plan(group * 3 + part, 0) for part in range(3)], tiles, code, mixed)
    own_sums, oth_sums = [], []
    for group in range(groups):
        pieces = range(group * 3, group * 3 + 3)
        for level in range(1, 3):
            for piece in pieces:
                half = held[piece].shape[0] // 2
                send = held[piece][half:] + arrived[piece][half:]
                held[piece] = held[piece][:half] + arrived[piece][:half]
                arrived[piece] = swap(send, steps[orders[piece % 3][level]])
        whole = jnp.concatenate(
            [(held[i] + arrived[i]).reshape(-1, counts[i] * tiles, LANES) for i in pieces], axis=1
        )
        for level in range(3, len(steps)):
            half = whole.shape[0] // 2
            whole = whole[:half] + swap(whole[half:], steps[level])
        own_sums.append(whole[0])
        oth_sums.append(swap(whole[0], core))

    half_rows = cols // 2
    sketch, product = pl.pallas_call(
        functools.partial(gram_kernel, 1.0 / math.sqrt(rows * devices), 1.0 / (samp * devices)),
        out_shape=[
            jax.ShapeDtypeStruct((samp, cols), jnp.float32),
            jax.ShapeDtypeStruct((half_rows, cols), jnp.float32),
        ],
        in_specs=[SMEM] + [VMEM] * (2 * groups),
        out_specs=[VMEM, VMEM],
        scratch_shapes=[pltpu.VMEM((2 * samp, cols), jnp.float32)],
        compiler_params=limit(8),
        cost_estimate=cost(24 * samp * samp * cols, 16 * samp * cols),
    )(lax.axis_index(core).astype(jnp.int32).reshape(1), *own_sums, *oth_sums)

    gram = reduce_gram(product.reshape(2, 2 ** len(low), -1, cols), high, low)
    return sketch, gram


def solution(mesh):
    width = [size.bit_length() - 1 for size in mesh.devices.shape]
    bits = [f"{axis}{i}" for axis, w in zip(mesh.axis_names, width) for i in reversed(range(w))]
    split = Mesh(mesh.devices.reshape((2,) * len(bits)), tuple(bits))
    every = tuple(bits)
    return jax.shard_map(
        functools.partial(per_device, bits),
        mesh=split,
        in_specs=(P(every, None), P(every), P(every)),
        out_specs=(P(every, None), P(every, None)),
        check_vma=False,
    )
```

```python
import functools
import math

import jax
import jax.numpy as jnp
from jax import lax
from jax.experimental import pallas as pl
from jax.experimental.pallas import tpu as pltpu
from jax.sharding import Mesh, PartitionSpec as P

HBM = pl.BlockSpec(memory_space=pltpu.HBM)
VMEM = pl.BlockSpec(memory_space=pltpu.VMEM)
SMEM = pl.BlockSpec(memory_space=pltpu.SMEM)
BLOCK = 256
LANES = 128
BATCH = 16
GROUPS = 1
CHUNKS = 4
NEGATIVE = 1 << 30


def limit(mib):
    return pltpu.CompilerParams(vmem_limit_bytes=mib * 1024 * 1024)


def cost(flops, moved):
    return pl.CostEstimate(flops=flops, bytes_accessed=moved, transcendentals=0)


def walsh(values):
    half = 1
    while half < len(values):
        out = list(values)
        for i in range(len(values)):
            if not i & half:
                out[i] = values[i] + values[i | half]
                out[i | half] = values[i] - values[i | half]
        values = out
        half *= 2
    return values


def transform_kernel(own_ref, oth_ref, own_sign_ref, oth_sign_ref, table_ref, held_ref, part_ref, sems):
    blocks, cols = part_ref.shape[1], part_ref.shape[3]
    tiles = cols // LANES
    chunk = blocks // CHUNKS
    copies = [
        pltpu.make_async_copy(
            ref.at[pl.ds(i * chunk * BLOCK, chunk * BLOCK)],
            held_ref.at[core, pl.ds(i * chunk * BLOCK, chunk * BLOCK)],
            sems.at[core, i],
        )
        for core, ref in enumerate((own_ref, oth_ref))
        for i in range(CHUNKS)
    ]
    for copy in copies:
        copy.start()
    common = lax.broadcasted_iota(jnp.int32, (BLOCK, BLOCK), 0) & lax.broadcasted_iota(
        jnp.int32, (BLOCK, BLOCK), 1
    )
    for shift in (4, 2, 1):
        common = common ^ (common >> shift)
    had = (1 - 2 * (common & 1)).astype(jnp.float32)
    for core, sign_ref in enumerate((own_sign_ref, oth_sign_ref)):
        for b in range(blocks):
            if b % chunk == 0:
                copies[core * CHUNKS + b // chunk].wait()
            left = (had * sign_ref[b : b + 1, :]).astype(jnp.bfloat16)
            full = held_ref[core, b * BLOCK : (b + 1) * BLOCK, :]
            high = full.astype(jnp.bfloat16)
            low = (full - high.astype(jnp.float32)).astype(jnp.bfloat16)
            part_ref[core, b] = jnp.dot(
                jnp.concatenate([left, left], axis=1),
                jnp.concatenate([high, low], axis=0),
                preferred_element_type=jnp.float32,
            )

    def one_chunk(chunk, carry):
        start = pl.multiple_of(chunk * 8, 8)
        for tile in range(tiles):
            lanes = slice(tile * LANES, (tile + 1) * LANES)
            own = walsh([part_ref[0, b, pl.ds(start, 8), lanes] for b in range(blocks)])
            oth = walsh([part_ref[1, b, pl.ds(start, 8), lanes] for b in range(blocks)])
            for b in range(blocks):
                for core, value in enumerate((own[b] + oth[b], own[b] - oth[b])):
                    row = (core * blocks + b) * BLOCK + start
                    table_ref[pl.ds(row * tiles + tile, 8, stride=tiles), :] = value
        return carry

    lax.fori_loop(0, BLOCK // 8, one_chunk, 0)


def transform(own, oth, own_sign, oth_sign):
    count, cols = own.shape
    blocks = count // BLOCK
    return pl.pallas_call(
        transform_kernel,
        out_shape=jax.ShapeDtypeStruct((2 * count * cols // LANES, LANES), jnp.float32),
        in_specs=[HBM, HBM, VMEM, VMEM],
        out_specs=VMEM,
        scratch_shapes=[
            pltpu.VMEM((2, count, cols), jnp.float32),
            pltpu.VMEM((2, blocks, BLOCK, cols), jnp.float32),
            pltpu.SemaphoreType.DMA((2, CHUNKS)),
        ],
        compiler_params=limit(18),
        cost_estimate=cost(8 * count * BLOCK * cols, 16 * count * cols),
    )(*(pltpu.with_memory_space_constraint(x, pltpu.HBM) for x in (own, oth)), own_sign, oth_sign)


def gather_kernel(plans, tiles, code_ref, table_ref, *out_refs):
    for out_ref, (starts, count) in zip(out_refs, plans):

        def copy(first, base, number, out_ref=out_ref):
            rows = []
            for i in range(number):
                code = code_ref[first + i]
                at = pl.multiple_of(code & (NEGATIVE - 1), tiles)
                row = table_ref[pl.ds(at, tiles), :]
                rows.append(jnp.where(code >= NEGATIVE, -row, row))
            for i, row in enumerate(rows):
                out_ref[pl.ds(pl.multiple_of((base + i) * tiles, tiles), tiles), :] = row

        for place, start in enumerate(starts):
            whole = count // BATCH

            def batch(step, carry, start=start, place=place, count=count, copy=copy):
                copy(start + step * BATCH, place * count + step * BATCH, BATCH)
                return carry

            lax.fori_loop(0, whole, batch, 0)
            if count % BATCH:
                copy(start + whole * BATCH, place * count + whole * BATCH, count % BATCH)


def gather(plans, tiles, code, table):
    total = sum(len(starts) * count for starts, count in plans)
    return pl.pallas_call(
        functools.partial(gather_kernel, plans, tiles),
        out_shape=[
            jax.ShapeDtypeStruct((len(starts) * count * tiles, LANES), jnp.float32)
            for starts, count in plans
        ],
        in_specs=[SMEM, VMEM],
        out_specs=[VMEM] * len(plans),
        compiler_params=limit(4),
        cost_estimate=cost(0, 8 * total * tiles * LANES),
    )(code, table)


def gram_kernel(scale, inverse_total, core_ref, *refs):
    sums, (sketch_ref, gram_ref, both_ref) = refs[:-3], refs[-3:]
    samp, cols = sketch_ref.shape
    tiles = cols // LANES
    for tile in range(tiles):
        lanes = slice(tile * LANES, (tile + 1) * LANES)
        at = 0
        for ref in sums:
            count = ref.shape[0] // tiles
            both_ref[at : at + count, lanes] = ref[pl.ds(tile, count, stride=tiles), :] * scale
            at += count
    sketch_ref[...] = both_ref[:samp, :]
    width = gram_ref.shape[0] // 2
    for upper in range(2):
        start = pl.multiple_of(upper * (cols // 2) + core_ref[0] * width, LANES)
        gram_ref[upper * width : (upper + 1) * width, :] = (
            lax.dot_general(
                both_ref[:, pl.ds(start, width)],
                both_ref[...],
                (((0,), (0,)), ((), ())),
                precision=lax.Precision.HIGHEST,
                preferred_element_type=jnp.float32,
            )
            * inverse_total
        )


def swap(block, bit):
    return lax.ppermute(block, bit, [(0, 1), (1, 0)])


def exclusive(block, place, axis):
    while block.shape[axis] > 1:
        half = block.shape[axis] // 2
        upper = lax.slice_in_dim(block, half, 2 * half, axis=axis)
        lower = lax.slice_in_dim(block, 0, half, axis=axis)
        block = jnp.where(place & half == half, upper, lower)
    return jnp.squeeze(block, axis)


def reduce_pairs(block, axes):
    own = lax.axis_index(axes)
    total = exclusive(block, own, 0)
    for flip in (3, 2, 1):
        route = [(i, i ^ flip) for i in range(4)]
        total += lax.ppermute(exclusive(block, own ^ flip, 0), axes, route)
    return total


def reduce_gram(block, high, low):
    first, rest = low[0], low[1:]
    block = block.reshape(2, -1, 2, *block.shape[2:])
    block = jnp.moveaxis(block, 2, 1).reshape(4, -1, *block.shape[3:])
    block = reduce_pairs(block, (high, first))
    while rest:
        if len(rest) >= 2:
            block = reduce_pairs(block.reshape(4, -1, *block.shape[1:]), (rest[-1], rest[-2]))
            rest = rest[:-2]
        else:
            last = rest[-1]
            own = lax.axis_index(last)
            block = block.reshape(2, -1, *block.shape[1:])
            block = exclusive(block, own, 0) + swap(exclusive(block, 1 - own, 0), last)
            rest = rest[:-1]
    return block[0]


def per_device(bits, design, signs, samples):
    rows, cols = design.shape
    samp = samples.shape[0]
    tiles = cols // LANES
    devices = 2 ** len(bits)
    high, core, low = bits[0], bits[1], bits[:1:-1]
    steps = [high, *low]
    own_index = lax.axis_index(tuple(bits))
    core_bit = len(low)

    oth_design = swap(design, core)
    oth_signs = swap(signs, core)
    sign_rows = [(2 * s - 1).astype(jnp.float32).reshape(rows // BLOCK, BLOCK) for s in (signs, oth_signs)]
    listing = steps
    listed = lax.optimization_barrier(samples ^ (own_index >> len(bits)))
    listed = jnp.concatenate([listed, swap(samples, listing[0])])
    for bit in listing[1:-1]:
        listed = jnp.concatenate([listed, swap(listed, bit)])
    listed, oth_design = lax.optimization_barrier((listed, oth_design))
    listed = jnp.concatenate([listed, swap(listed, listing[-1])])
    mixed = transform(design, oth_design, *sign_rows)

    source = listed // rows
    parity = source & own_index
    shift = 1
    while shift < devices:
        parity = parity ^ (parity >> shift)
        shift *= 2
    code = ((source >> core_bit & 1) * rows + listed % rows) * tiles + (parity & 1) * NEGATIVE

    owners = devices // 2
    groups = GROUPS
    group_samp = samp // groups
    third = (group_samp // 3 + 2) // 2 * 2
    counts = [third, third, group_samp - 2 * third] * groups
    orders = []
    for part in range(3):
        order = [(part + i) % 3 for i in range(3)]
        orders.append(order + list(range(3, len(steps))))

    def plan(piece, first):
        order = orders[piece % 3]
        found = []
        for place in range(owners // 2):
            owner = first << listing.index(steps[order[0]])
            for level, bit in enumerate(order[1:]):
                owner |= (place >> (len(order) - 2 - level) & 1) << listing.index(steps[bit])
            found.append(owner * samp + sum(counts[:piece]))
        return found, counts[piece]

    arrived, held = [], []
    for group in range(groups):
        pieces = range(group * 3, group * 3 + 3)
        sent = gather([plan(piece, 1) for piece in pieces], tiles, code, mixed)
        arrived += [swap(rows_sent, steps[part]) for part, rows_sent in enumerate(sent)]
    for group in range(groups):
        held += gather([plan(group * 3 + part, 0) for part in range(3)], tiles, code, mixed)
    own_sums, oth_sums = [], []
    for group in range(groups):
        pieces = range(group * 3, group * 3 + 3)
        for level in range(1, 3):
            for piece in pieces:
                half = held[piece].shape[0] // 2
                send = held[piece][half:] + arrived[piece][half:]
                held[piece] = held[piece][:half] + arrived[piece][:half]
                arrived[piece] = swap(send, steps[orders[piece % 3][level]])
        whole = jnp.concatenate(
            [(held[i] + arrived[i]).reshape(-1, counts[i] * tiles, LANES) for i in pieces], axis=1
        )
        for level in range(3, len(steps)):
            half = whole.shape[0] // 2
            whole = whole[:half] + swap(whole[half:], steps[level])
        own_sums.append(whole[0])
        oth_sums.append(swap(whole[0], core))

    half_rows = cols // 2
    sketch, product = pl.pallas_call(
        functools.partial(gram_kernel, 1.0 / math.sqrt(rows * devices), 1.0 / (samp * devices)),
        out_shape=[
            jax.ShapeDtypeStruct((samp, cols), jnp.float32),
            jax.ShapeDtypeStruct((half_rows, cols), jnp.float32),
        ],
        in_specs=[SMEM] + [VMEM] * (2 * groups),
        out_specs=[VMEM, VMEM],
        scratch_shapes=[pltpu.VMEM((2 * samp, cols), jnp.float32)],
        compiler_params=limit(8),
        cost_estimate=cost(24 * samp * samp * cols, 16 * samp * cols),
    )(lax.axis_index(core).astype(jnp.int32).reshape(1), *own_sums, *oth_sums)

    gram = reduce_gram(product.reshape(2, 2 ** len(low), -1, cols), high, low)
    return sketch, gram


def solution(mesh):
    width = [size.bit_length() - 1 for size in mesh.devices.shape]
    bits = [f"{axis}{i}" for axis, w in zip(mesh.axis_names, width) for i in reversed(range(w))]
    split = Mesh(mesh.devices.reshape((2,) * len(bits)), tuple(bits))
    every = tuple(bits)
    return jax.shard_map(
        functools.partial(per_device, bits),
        mesh=split,
        in_specs=(P(every, None), P(every), P(every)),
        out_specs=(P(every, None), P(every, None)),
        check_vma=False,
    )
```

```python
import functools
import math

import jax
import jax.numpy as jnp
from jax import lax
from jax.experimental import pallas as pl
from jax.experimental.pallas import tpu as pltpu
from jax.sharding import Mesh, PartitionSpec as P

HBM = pl.BlockSpec(memory_space=pltpu.HBM)
VMEM = pl.BlockSpec(memory_space=pltpu.VMEM)
SMEM = pl.BlockSpec(memory_space=pltpu.SMEM)
BLOCK = 256
LANES = 128
CHUNKS = 2


def limit(mib):
    return pltpu.CompilerParams(vmem_limit_bytes=mib * 1024 * 1024)


def cost(flops, moved):
    return pl.CostEstimate(flops=flops, bytes_accessed=moved, transcendentals=0)


def walsh(values):
    half = 1
    while half < len(values):
        out = list(values)
        for i in range(len(values)):
            if not i & half:
                out[i] = values[i] + values[i | half]
                out[i | half] = values[i] - values[i | half]
        values = out
        half *= 2
    return values


def blocks_kernel(rows_ref, sign_ref, part_ref, zero_ref, held_ref, sems):
    zero_ref[...] = jnp.zeros_like(zero_ref)
    blocks = part_ref.shape[0]
    chunk = blocks // CHUNKS
    copies = []
    for i in range(CHUNKS):
        window = pl.ds(i * chunk * BLOCK, chunk * BLOCK)
        copies.append(pltpu.make_async_copy(rows_ref.at[window], held_ref.at[window], sems.at[i]))
        copies[i].start()
    common = lax.broadcasted_iota(jnp.int32, (BLOCK, BLOCK), 0) & lax.broadcasted_iota(
        jnp.int32, (BLOCK, BLOCK), 1
    )
    for shift in (4, 2, 1):
        common = common ^ (common >> shift)
    had = (1 - 2 * (common & 1)).astype(jnp.float32)
    for b in range(blocks):
        if b % chunk == 0:
            copies[b // chunk].wait()
        left = (had * sign_ref[b : b + 1, :]).astype(jnp.bfloat16)
        full = held_ref[b * BLOCK : (b + 1) * BLOCK, :]
        high = full.astype(jnp.bfloat16)
        low = (full - high.astype(jnp.float32)).astype(jnp.bfloat16)
        part_ref[b] = jnp.dot(
            jnp.concatenate([left, left], axis=1),
            jnp.concatenate([high, low], axis=0),
            preferred_element_type=jnp.float32,
        )


def transform_blocks(rows, sign, length):
    count, cols = rows.shape
    blocks = count // BLOCK
    return pl.pallas_call(
        blocks_kernel,
        out_shape=[
            jax.ShapeDtypeStruct((blocks, BLOCK, cols), jnp.float32),
            jax.ShapeDtypeStruct((length,), jnp.int32),
        ],
        in_specs=[HBM, VMEM],
        out_specs=[VMEM, VMEM],
        scratch_shapes=[pltpu.VMEM((count, cols), jnp.float32), pltpu.SemaphoreType.DMA((CHUNKS,))],
        compiler_params=limit(8),
        cost_estimate=cost(4 * count * BLOCK * cols, 8 * count * cols),
    )(pltpu.with_memory_space_constraint(rows, pltpu.HBM), sign)


def merge_kernel(own_ref, oth_ref, table_ref):
    blocks, _, cols = own_ref.shape
    tiles = cols // LANES

    def one_chunk(step, carry):
        start = pl.multiple_of(step * 8, 8)
        for tile in range(tiles):
            lanes = slice(tile * LANES, (tile + 1) * LANES)
            own = walsh([own_ref[b, pl.ds(start, 8), lanes] for b in range(blocks)])
            oth = walsh([oth_ref[b, pl.ds(start, 8), lanes] for b in range(blocks)])
            for b in range(blocks):
                for core, value in enumerate((own[b] + oth[b], own[b] - oth[b])):
                    row = (core * blocks + b) * BLOCK + start
                    table_ref[pl.ds(row * tiles + tile, 8, stride=tiles), :] = value
        return carry

    lax.fori_loop(0, BLOCK // 8, one_chunk, 0)


def merge(own, oth):
    blocks, _, cols = own.shape
    return pl.pallas_call(
        merge_kernel,
        out_shape=jax.ShapeDtypeStruct((2 * blocks * BLOCK * cols // LANES, LANES), jnp.float32),
        in_specs=[VMEM, VMEM],
        out_specs=VMEM,
        compiler_params=limit(4),
        cost_estimate=cost(10 * blocks * BLOCK * cols, 16 * blocks * BLOCK * cols),
    )(own, oth)


def gather_kernel(plans, tiles, at_ref, sign_ref, table_ref, *out_refs):
    for out_ref, (fixed, places, skip, count) in zip(out_refs, plans):

        def one_owner(place, carry, out_ref=out_ref, fixed=fixed, places=places, skip=skip, count=count):
            owner = fixed
            for i, bit in enumerate(places):
                owner = owner + ((place >> i & 1) << bit)
            first = owner * count[0] + skip
            rows = []
            for i in range(count[1]):
                at = pl.multiple_of(at_ref[first + i], tiles)
                rows.append(table_ref[pl.ds(at, tiles), :] * sign_ref[first + i])
            for i, row in enumerate(rows):
                to = pl.multiple_of((place * count[1] + i) * tiles, tiles)
                out_ref[pl.ds(to, tiles), :] = row
            return carry

        lax.fori_loop(0, 2 ** len(places), one_owner, 0)


def gather(plans, tiles, at, sign, table):
    total = [2 ** len(places) * count[1] for _, places, _, count in plans]
    return pl.pallas_call(
        functools.partial(gather_kernel, plans, tiles),
        out_shape=[jax.ShapeDtypeStruct((rows * tiles, LANES), jnp.float32) for rows in total],
        in_specs=[SMEM, SMEM, VMEM],
        out_specs=[VMEM] * len(plans),
        compiler_params=limit(4),
        cost_estimate=cost(0, 8 * sum(total) * tiles * LANES),
    )(at, sign, table)


def gram_kernel(scale, inverse_total, core_ref, own_ref, oth_ref, sketch_ref, gram_ref, high_ref, low_ref):
    samp, cols = sketch_ref.shape
    tiles = cols // LANES
    for which, ref in enumerate((own_ref, oth_ref)):
        for tile in range(tiles):
            lanes = slice(tile * LANES, (tile + 1) * LANES)
            value = ref[pl.ds(tile, samp, stride=tiles), :] * scale
            if not which:
                sketch_ref[:, lanes] = value
            high = value.astype(jnp.bfloat16)
            high_ref[which * samp : (which + 1) * samp, lanes] = high
            low_ref[which * samp : (which + 1) * samp, lanes] = (
                value - high.astype(jnp.float32)
            ).astype(jnp.bfloat16)
    width = gram_ref.shape[0] // 2
    for upper in range(2):
        start = pl.multiple_of(upper * (cols // 2) + core_ref[0] * width, LANES)
        total = None
        for left_ref, right_ref in ((high_ref, high_ref), (high_ref, low_ref), (low_ref, high_ref)):
            term = lax.dot_general(
                left_ref[:, pl.ds(start, width)],
                right_ref[...],
                (((0,), (0,)), ((), ())),
                preferred_element_type=jnp.float32,
            )
            total = term if total is None else total + term
        gram_ref[upper * width : (upper + 1) * width, :] = total * inverse_total


def swap(block, bit):
    return lax.ppermute(block, bit, [(0, 1), (1, 0)])


def exclusive(block, place, axis):
    while block.shape[axis] > 1:
        half = block.shape[axis] // 2
        upper = lax.slice_in_dim(block, half, 2 * half, axis=axis)
        lower = lax.slice_in_dim(block, 0, half, axis=axis)
        block = jnp.where(place & half == half, upper, lower)
    return jnp.squeeze(block, axis)


def reduce_pairs(block, axes):
    own = lax.axis_index(axes)
    total = exclusive(block, own, 0)
    for flip in (3, 2, 1):
        route = [(i, i ^ flip) for i in range(4)]
        total += lax.ppermute(exclusive(block, own ^ flip, 0), axes, route)
    return total


def reduce_gram(block, high, low):
    first, rest = low[0], low[1:]
    block = block.reshape(2, -1, 2, *block.shape[2:])
    block = jnp.moveaxis(block, 2, 1).reshape(4, -1, *block.shape[3:])
    block = reduce_pairs(block, (high, first))
    while rest:
        if len(rest) >= 2:
            block = reduce_pairs(block.reshape(4, -1, *block.shape[1:]), (rest[-1], rest[-2]))
            rest = rest[:-2]
        else:
            last = rest[-1]
            own = lax.axis_index(last)
            block = block.reshape(2, -1, *block.shape[1:])
            block = exclusive(block, own, 0) + swap(exclusive(block, 1 - own, 0), last)
            rest = rest[:-1]
    return block[0]


def per_device(bits, design, signs, samples):
    rows, cols = design.shape
    samp = samples.shape[0]
    tiles = cols // LANES
    devices = 2 ** len(bits)
    high, core, low = bits[0], bits[1], bits[:1:-1]
    steps = [high, *low]
    own_index = lax.axis_index(tuple(bits))
    core_bit = len(low)

    own_sign = (2 * signs - 1).astype(jnp.float32).reshape(rows // BLOCK, BLOCK)
    oth_design = swap(design, core)
    oth_sign = swap(own_sign, core)
    listing = steps
    listed = lax.optimization_barrier(samples ^ (own_index >> len(bits)))
    listed = jnp.concatenate([listed, swap(samples, listing[0])])
    for i, bit in enumerate(listing[1:], 1):
        listed = jnp.concatenate([listed, swap(listed, bit)])
        if i == 1:
            own_blocks, zeros = transform_blocks(design, own_sign, listed.shape[0])
            listed = listed + zeros
        if i == len(steps) - 2:
            oth_blocks, zeros = transform_blocks(oth_design, oth_sign, listed.shape[0])
            listed = listed + zeros
    mixed = merge(own_blocks, oth_blocks)

    source = listed // rows
    parity = source & own_index
    shift = 1
    while shift < devices:
        parity = parity ^ (parity >> shift)
        shift *= 2
    at = ((source >> core_bit & 1) * rows + listed % rows) * tiles
    sign = (1 - 2 * (parity & 1)).astype(jnp.float32)

    third = (samp // 3 + 2) // 2 * 2
    counts = [third, third, samp - 2 * third]
    orders = []
    for part in range(3):
        order = [(part + i) % 3 for i in range(3)]
        orders.append(order + list(range(3, len(steps))))

    def plan(part, first):
        places = [listing.index(steps[bit]) for bit in orders[part]]
        return first << places[0], places[:0:-1], sum(counts[:part]), (samp, counts[part])

    parts = range(3)
    sent = gather([plan(part, 1) for part in parts], tiles, at, sign, mixed)
    arrived = [swap(sent[part], steps[part]) for part in parts]
    held = list(gather([plan(part, 0) for part in parts], tiles, at, sign, mixed))
    for level in range(1, 3):
        for part in parts:
            half = held[part].shape[0] // 2
            send = held[part][half:] + arrived[part][half:]
            held[part] = held[part][:half] + arrived[part][:half]
            arrived[part] = swap(send, steps[orders[part][level]])
    done = []
    for members in ((2,), (0, 1)):
        whole = jnp.concatenate(
            [(held[part] + arrived[part]).reshape(-1, counts[part] * tiles, LANES) for part in members], axis=1
        )
        for level in range(3, len(steps)):
            half = whole.shape[0] // 2
            whole = whole[:half] + swap(whole[half:], steps[level])
        done.append(whole[0])
    own_sum = jnp.concatenate([done[1], done[0]])
    oth_sum = swap(own_sum, core)

    half_rows = cols // 2
    sketch, product = pl.pallas_call(
        functools.partial(gram_kernel, 1.0 / math.sqrt(rows * devices), 1.0 / (samp * devices)),
        out_shape=[
            jax.ShapeDtypeStruct((samp, cols), jnp.float32),
            jax.ShapeDtypeStruct((half_rows, cols), jnp.float32),
        ],
        in_specs=[SMEM] + [VMEM] * 2,
        out_specs=[VMEM, VMEM],
        scratch_shapes=[pltpu.VMEM((2 * samp, cols), jnp.bfloat16)] * 2,
        compiler_params=limit(8),
        cost_estimate=cost(24 * samp * samp * cols, 16 * samp * cols),
    )(lax.axis_index(core).astype(jnp.int32).reshape(1), own_sum, oth_sum)

    gram = reduce_gram(product.reshape(2, 2 ** len(low), -1, cols), high, low)
    return sketch, gram


def solution(mesh):
    width = [size.bit_length() - 1 for size in mesh.devices.shape]
    bits = [f"{axis}{i}" for axis, w in zip(mesh.axis_names, width) for i in reversed(range(w))]
    split = Mesh(mesh.devices.reshape((2,) * len(bits)), tuple(bits))
    every = tuple(bits)
    return jax.shard_map(
        functools.partial(per_device, bits),
        mesh=split,
        in_specs=(P(every, None), P(every), P(every)),
        out_specs=(P(every, None), P(every, None)),
        check_vma=False,
    )
```

```python
import functools
import math

import jax
import jax.numpy as jnp
from jax import lax
from jax.experimental import pallas as pl
from jax.experimental.pallas import tpu as pltpu
from jax.sharding import Mesh, PartitionSpec as P

HBM = pl.BlockSpec(memory_space=pltpu.HBM)
VMEM = pl.BlockSpec(memory_space=pltpu.VMEM)
SMEM = pl.BlockSpec(memory_space=pltpu.SMEM)
BLOCK = 256
LANES = 128
CHUNKS = 2


def limit(mib):
    return pltpu.CompilerParams(vmem_limit_bytes=mib * 1024 * 1024)


def cost(flops, moved):
    return pl.CostEstimate(flops=flops, bytes_accessed=moved, transcendentals=0)


def walsh(values):
    half = 1
    while half < len(values):
        out = list(values)
        for i in range(len(values)):
            if not i & half:
                out[i] = values[i] + values[i | half]
                out[i | half] = values[i] - values[i | half]
        values = out
        half *= 2
    return values


def blocks_kernel(rows_ref, sign_ref, part_ref, zero_ref, held_ref, sems):
    zero_ref[...] = jnp.zeros_like(zero_ref)
    blocks = part_ref.shape[0]
    chunk = blocks // CHUNKS
    copies = []
    for i in range(CHUNKS):
        window = pl.ds(i * chunk * BLOCK, chunk * BLOCK)
        copies.append(pltpu.make_async_copy(rows_ref.at[window], held_ref.at[window], sems.at[i]))
        copies[i].start()
    common = lax.broadcasted_iota(jnp.int32, (BLOCK, BLOCK), 0) & lax.broadcasted_iota(
        jnp.int32, (BLOCK, BLOCK), 1
    )
    for shift in (4, 2, 1):
        common = common ^ (common >> shift)
    had = (1 - 2 * (common & 1)).astype(jnp.float32)
    for b in range(blocks):
        if b % chunk == 0:
            copies[b // chunk].wait()
        left = (had * sign_ref[b : b + 1, :]).astype(jnp.bfloat16)
        full = held_ref[b * BLOCK : (b + 1) * BLOCK, :]
        high = full.astype(jnp.bfloat16)
        low = (full - high.astype(jnp.float32)).astype(jnp.bfloat16)
        part_ref[b] = jnp.dot(
            jnp.concatenate([left, left], axis=1),
            jnp.concatenate([high, low], axis=0),
            preferred_element_type=jnp.float32,
        )


def transform_blocks(rows, sign, length):
    count, cols = rows.shape
    blocks = count // BLOCK
    return pl.pallas_call(
        blocks_kernel,
        out_shape=[
            jax.ShapeDtypeStruct((blocks, BLOCK, cols), jnp.float32),
            jax.ShapeDtypeStruct((length,), jnp.int32),
        ],
        in_specs=[HBM, VMEM],
        out_specs=[VMEM, VMEM],
        scratch_shapes=[pltpu.VMEM((count, cols), jnp.float32), pltpu.SemaphoreType.DMA((CHUNKS,))],
        compiler_params=limit(8),
        cost_estimate=cost(4 * count * BLOCK * cols, 8 * count * cols),
    )(pltpu.with_memory_space_constraint(rows, pltpu.HBM), sign)


def merge_kernel(own_ref, oth_ref, table_ref):
    blocks, _, cols = own_ref.shape
    tiles = cols // LANES

    def one_chunk(step, carry):
        start = pl.multiple_of(step * 8, 8)
        for tile in range(tiles):
            lanes = slice(tile * LANES, (tile + 1) * LANES)
            own = walsh([own_ref[b, pl.ds(start, 8), lanes] for b in range(blocks)])
            oth = walsh([oth_ref[b, pl.ds(start, 8), lanes] for b in range(blocks)])
            for b in range(blocks):
                for core, value in enumerate((own[b] + oth[b], own[b] - oth[b])):
                    row = (core * blocks + b) * BLOCK + start
                    table_ref[pl.ds(row * tiles + tile, 8, stride=tiles), :] = value
        return carry

    lax.fori_loop(0, BLOCK // 8, one_chunk, 0)


def merge(own, oth):
    blocks, _, cols = own.shape
    return pl.pallas_call(
        merge_kernel,
        out_shape=jax.ShapeDtypeStruct((2 * blocks * BLOCK * cols // LANES, LANES), jnp.float32),
        in_specs=[VMEM, VMEM],
        out_specs=VMEM,
        compiler_params=limit(4),
        cost_estimate=cost(10 * blocks * BLOCK * cols, 16 * blocks * BLOCK * cols),
    )(own, oth)


def gather_kernel(plans, tiles, at_ref, sign_ref, table_ref, *out_refs):
    for out_ref, (fixed, places, skip, count) in zip(out_refs, plans):

        def one_owner(place, carry, out_ref=out_ref, fixed=fixed, places=places, skip=skip, count=count):
            owner = fixed
            for i, bit in enumerate(places):
                owner = owner + ((place >> i & 1) << bit)
            first = owner * count[0] + skip
            rows = []
            for i in range(count[1]):
                at = pl.multiple_of(at_ref[first + i], tiles)
                rows.append(table_ref[pl.ds(at, tiles), :] * sign_ref[first + i])
            for i, row in enumerate(rows):
                to = pl.multiple_of((place * count[1] + i) * tiles, tiles)
                out_ref[pl.ds(to, tiles), :] = row
            return carry

        lax.fori_loop(0, 2 ** len(places), one_owner, 0)


def gather(plans, tiles, at, sign, table):
    total = [2 ** len(places) * count[1] for _, places, _, count in plans]
    return pl.pallas_call(
        functools.partial(gather_kernel, plans, tiles),
        out_shape=[jax.ShapeDtypeStruct((rows * tiles, LANES), jnp.float32) for rows in total],
        in_specs=[SMEM, SMEM, VMEM],
        out_specs=[VMEM] * len(plans),
        compiler_params=limit(4),
        cost_estimate=cost(0, 8 * sum(total) * tiles * LANES),
    )(at, sign, table)


def gram_kernel(scale, inverse_total, core_ref, own_ref, oth_ref, sketch_ref, gram_ref, high_ref, low_ref):
    samp, cols = sketch_ref.shape
    tiles = cols // LANES
    for which, ref in enumerate((own_ref, oth_ref)):
        for tile in range(tiles):
            lanes = slice(tile * LANES, (tile + 1) * LANES)
            value = ref[pl.ds(tile, samp, stride=tiles), :] * scale
            if not which:
                sketch_ref[:, lanes] = value
            high = value.astype(jnp.bfloat16)
            high_ref[which * samp : (which + 1) * samp, lanes] = high
            low_ref[which * samp : (which + 1) * samp, lanes] = (
                value - high.astype(jnp.float32)
            ).astype(jnp.bfloat16)
    width = gram_ref.shape[0] // 2
    for upper in range(2):
        start = pl.multiple_of(upper * (cols // 2) + core_ref[0] * width, LANES)
        total = None
        for left_ref, right_ref in ((high_ref, high_ref), (high_ref, low_ref), (low_ref, high_ref)):
            term = lax.dot_general(
                left_ref[:, pl.ds(start, width)],
                right_ref[...],
                (((0,), (0,)), ((), ())),
                preferred_element_type=jnp.float32,
            )
            total = term if total is None else total + term
        gram_ref[upper * width : (upper + 1) * width, :] = total * inverse_total


def swap(block, bit):
    return lax.ppermute(block, bit, [(0, 1), (1, 0)])


def exclusive(block, place, axis):
    while block.shape[axis] > 1:
        half = block.shape[axis] // 2
        upper = lax.slice_in_dim(block, half, 2 * half, axis=axis)
        lower = lax.slice_in_dim(block, 0, half, axis=axis)
        block = jnp.where(place & half == half, upper, lower)
    return jnp.squeeze(block, axis)


def reduce_pairs(block, axes):
    own = lax.axis_index(axes)
    total = exclusive(block, own, 0)
    for flip in (3, 2, 1):
        route = [(i, i ^ flip) for i in range(4)]
        total += lax.ppermute(exclusive(block, own ^ flip, 0), axes, route)
    return total


def reduce_gram(block, high, low):
    first, rest = low[0], low[1:]
    block = block.reshape(2, -1, 2, *block.shape[2:])
    block = jnp.moveaxis(block, 2, 1).reshape(4, -1, *block.shape[3:])
    block = reduce_pairs(block, (high, first))
    while rest:
        if len(rest) >= 2:
            block = reduce_pairs(block.reshape(4, -1, *block.shape[1:]), (rest[-1], rest[-2]))
            rest = rest[:-2]
        else:
            last = rest[-1]
            own = lax.axis_index(last)
            block = block.reshape(2, -1, *block.shape[1:])
            block = exclusive(block, own, 0) + swap(exclusive(block, 1 - own, 0), last)
            rest = rest[:-1]
    return block[0]


def per_device(bits, design, signs, samples):
    rows, cols = design.shape
    samp = samples.shape[0]
    tiles = cols // LANES
    devices = 2 ** len(bits)
    high, core, low = bits[0], bits[1], bits[:1:-1]
    steps = [high, *low]
    own_index = lax.axis_index(tuple(bits))
    core_bit = len(low)

    own_sign = (2 * signs - 1).astype(jnp.float32).reshape(rows // BLOCK, BLOCK)
    oth_design = swap(design, core)
    oth_sign = swap(own_sign, core)
    listing = steps
    listed = lax.optimization_barrier(samples ^ (own_index >> len(bits)))
    listed = jnp.concatenate([listed, swap(samples, listing[0])])
    for i, bit in enumerate(listing[1:], 1):
        listed = jnp.concatenate([listed, swap(listed, bit)])
        if i == 1:
            own_blocks, zeros = transform_blocks(design, own_sign, listed.shape[0])
            listed = listed + zeros
        if i == len(steps) - 2:
            oth_blocks, zeros = transform_blocks(oth_design, oth_sign, listed.shape[0])
            listed = listed + zeros
    mixed = merge(own_blocks, oth_blocks)

    source = listed // rows
    parity = source & own_index
    shift = 1
    while shift < devices:
        parity = parity ^ (parity >> shift)
        shift *= 2
    at = ((source >> core_bit & 1) * rows + listed % rows) * tiles
    sign = (1 - 2 * (parity & 1)).astype(jnp.float32)

    third = samp // 6 * 2
    counts = [third + 0, third + 0]
    counts.append(samp - sum(counts))
    orders = []
    for part in range(3):
        order = [(part + i) % 3 for i in range(3)]
        orders.append(order + list(range(3, len(steps))))

    def plan(part, first):
        places = [listing.index(steps[bit]) for bit in orders[part]]
        return first << places[0], places[:0:-1], sum(counts[:part]), (samp, counts[part])

    parts = range(3)
    sent = gather([plan(part, 1) for part in parts], tiles, at, sign, mixed)
    arrived = [swap(sent[part], steps[part]) for part in parts]
    held = list(gather([plan(part, 0) for part in parts], tiles, at, sign, mixed))
    for level in range(1, 3):
        for part in parts:
            half = held[part].shape[0] // 2
            send = held[part][half:] + arrived[part][half:]
            held[part] = held[part][:half] + arrived[part][:half]
            arrived[part] = swap(send, steps[orders[part][level]])
    done = []
    for members in ((2,), (0,), (1,)):
        whole = jnp.concatenate(
            [(held[part] + arrived[part]).reshape(-1, counts[part] * tiles, LANES) for part in members], axis=1
        )
        for level in range(3, len(steps)):
            half = whole.shape[0] // 2
            whole = whole[:half] + swap(whole[half:], steps[level])
        done.append(whole[0])
    own_sum = jnp.concatenate([done[1], done[2], done[0]])
    oth_sum = swap(own_sum, core)

    half_rows = cols // 2
    sketch, product = pl.pallas_call(
        functools.partial(gram_kernel, 1.0 / math.sqrt(rows * devices), 1.0 / (samp * devices)),
        out_shape=[
            jax.ShapeDtypeStruct((samp, cols), jnp.float32),
            jax.ShapeDtypeStruct((half_rows, cols), jnp.float32),
        ],
        in_specs=[SMEM] + [VMEM] * 2,
        out_specs=[VMEM, VMEM],
        scratch_shapes=[pltpu.VMEM((2 * samp, cols), jnp.bfloat16)] * 2,
        compiler_params=limit(8),
        cost_estimate=cost(24 * samp * samp * cols, 16 * samp * cols),
    )(lax.axis_index(core).astype(jnp.int32).reshape(1), own_sum, oth_sum)

    gram = reduce_gram(product.reshape(2, 2 ** len(low), -1, cols), high, low)
    return sketch, gram


def solution(mesh):
    width = [size.bit_length() - 1 for size in mesh.devices.shape]
    bits = [f"{axis}{i}" for axis, w in zip(mesh.axis_names, width) for i in reversed(range(w))]
    split = Mesh(mesh.devices.reshape((2,) * len(bits)), tuple(bits))
    every = tuple(bits)
    return jax.shard_map(
        functools.partial(per_device, bits),
        mesh=split,
        in_specs=(P(every, None), P(every), P(every)),
        out_specs=(P(every, None), P(every, None)),
        check_vma=False,
    )
```

```python
import functools
import math

import jax
import jax.numpy as jnp
from jax import lax
from jax.experimental import pallas as pl
from jax.experimental.pallas import tpu as pltpu
from jax.sharding import Mesh, PartitionSpec as P

HBM = pl.BlockSpec(memory_space=pltpu.HBM)
VMEM = pl.BlockSpec(memory_space=pltpu.VMEM)
SMEM = pl.BlockSpec(memory_space=pltpu.SMEM)
BLOCK = 256
LANES = 128
CHUNKS = 2


def limit(mib):
    return pltpu.CompilerParams(vmem_limit_bytes=mib * 1024 * 1024)


def cost(flops, moved):
    return pl.CostEstimate(flops=flops, bytes_accessed=moved, transcendentals=0)


def walsh(values):
    half = 1
    while half < len(values):
        out = list(values)
        for i in range(len(values)):
            if not i & half:
                out[i] = values[i] + values[i | half]
                out[i | half] = values[i] - values[i | half]
        values = out
        half *= 2
    return values


def blocks_kernel(rows_ref, sign_ref, part_ref, zero_ref, held_ref, sems):
    zero_ref[...] = jnp.zeros_like(zero_ref)
    blocks = part_ref.shape[0]
    chunk = blocks // CHUNKS
    copies = []
    for i in range(CHUNKS):
        window = pl.ds(i * chunk * BLOCK, chunk * BLOCK)
        copies.append(pltpu.make_async_copy(rows_ref.at[window], held_ref.at[window], sems.at[i]))
        copies[i].start()
    common = lax.broadcasted_iota(jnp.int32, (BLOCK, BLOCK), 0) & lax.broadcasted_iota(
        jnp.int32, (BLOCK, BLOCK), 1
    )
    for shift in (4, 2, 1):
        common = common ^ (common >> shift)
    had = (1 - 2 * (common & 1)).astype(jnp.float32)
    for b in range(blocks):
        if b % chunk == 0:
            copies[b // chunk].wait()
        left = (had * sign_ref[b : b + 1, :]).astype(jnp.bfloat16)
        full = held_ref[b * BLOCK : (b + 1) * BLOCK, :]
        high = full.astype(jnp.bfloat16)
        low = (full - high.astype(jnp.float32)).astype(jnp.bfloat16)
        part_ref[b] = jnp.dot(
            jnp.concatenate([left, left], axis=1),
            jnp.concatenate([high, low], axis=0),
            preferred_element_type=jnp.float32,
        )


def transform_blocks(rows, sign, length):
    count, cols = rows.shape
    blocks = count // BLOCK
    return pl.pallas_call(
        blocks_kernel,
        out_shape=[
            jax.ShapeDtypeStruct((blocks, BLOCK, cols), jnp.float32),
            jax.ShapeDtypeStruct((length,), jnp.int32),
        ],
        in_specs=[HBM, VMEM],
        out_specs=[VMEM, VMEM],
        scratch_shapes=[pltpu.VMEM((count, cols), jnp.float32), pltpu.SemaphoreType.DMA((CHUNKS,))],
        compiler_params=limit(8),
        cost_estimate=cost(4 * count * BLOCK * cols, 8 * count * cols),
    )(pltpu.with_memory_space_constraint(rows, pltpu.HBM), sign)


def merge_kernel(own_ref, oth_ref, table_ref):
    blocks, _, cols = own_ref.shape
    tiles = cols // LANES

    def one_chunk(step, carry):
        start = pl.multiple_of(step * 8, 8)
        for tile in range(tiles):
            lanes = slice(tile * LANES, (tile + 1) * LANES)
            own = walsh([own_ref[b, pl.ds(start, 8), lanes] for b in range(blocks)])
            oth = walsh([oth_ref[b, pl.ds(start, 8), lanes] for b in range(blocks)])
            for b in range(blocks):
                for core, value in enumerate((own[b] + oth[b], own[b] - oth[b])):
                    row = (core * blocks + b) * BLOCK + start
                    table_ref[pl.ds(row * tiles + tile, 8, stride=tiles), :] = value
        return carry

    lax.fori_loop(0, BLOCK // 8, one_chunk, 0)


def merge(own, oth):
    blocks, _, cols = own.shape
    tiles = cols // LANES
    return pl.pallas_call(
        merge_kernel,
        out_shape=jax.ShapeDtypeStruct((2 * blocks * BLOCK * tiles + 8, LANES), jnp.float32),
        in_specs=[VMEM, VMEM],
        out_specs=VMEM,
        compiler_params=limit(4),
        cost_estimate=cost(10 * blocks * BLOCK * cols, 16 * blocks * BLOCK * cols),
    )(own, oth)


def gather_kernel(plans, tiles, at_ref, sign_ref, table_ref, *out_refs):
    for out_ref, (fixed, places, skip, count) in zip(out_refs, plans):

        def one_owner(place, carry, out_ref=out_ref, fixed=fixed, places=places, skip=skip, count=count):
            owner = fixed
            for i, bit in enumerate(places):
                owner = owner + ((place >> i & 1) << bit)
            first = owner * count[0] + skip
            rows = []
            for i in range(count[1]):
                at = pl.multiple_of(at_ref[first + i], tiles)
                rows.append(table_ref[pl.ds(at, tiles), :] * sign_ref[first + i])
            for i, row in enumerate(rows):
                to = pl.multiple_of((place * count[1] + i) * tiles, tiles)
                out_ref[pl.ds(to, tiles), :] = row
            return carry

        lax.fori_loop(0, 2 ** len(places), one_owner, 0)


def gather(plans, tiles, at, sign, table):
    total = [2 ** len(places) * count[1] for _, places, _, count in plans]
    return pl.pallas_call(
        functools.partial(gather_kernel, plans, tiles),
        out_shape=[jax.ShapeDtypeStruct((rows * tiles, LANES), jnp.float32) for rows in total],
        in_specs=[SMEM, SMEM, VMEM],
        out_specs=[VMEM] * len(plans),
        compiler_params=limit(4),
        cost_estimate=cost(0, 8 * sum(total) * tiles * LANES),
    )(at, sign, table)


def gram_kernel(scale, inverse_total, core_ref, own_ref, oth_ref, sketch_ref, gram_ref, high_ref, low_ref):
    samp, cols = sketch_ref.shape
    tiles = cols // LANES
    for which, ref in enumerate((own_ref, oth_ref)):
        for tile in range(tiles):
            lanes = slice(tile * LANES, (tile + 1) * LANES)
            value = ref[pl.ds(tile, samp, stride=tiles), :] * scale
            if not which:
                sketch_ref[:, lanes] = value
            high = value.astype(jnp.bfloat16)
            high_ref[which * samp : (which + 1) * samp, lanes] = high
            low_ref[which * samp : (which + 1) * samp, lanes] = (
                value - high.astype(jnp.float32)
            ).astype(jnp.bfloat16)
    width = gram_ref.shape[0] // 2
    for upper in range(2):
        start = pl.multiple_of(upper * (cols // 2) + core_ref[0] * width, LANES)
        total = None
        for left_ref, right_ref in ((high_ref, high_ref), (high_ref, low_ref), (low_ref, high_ref)):
            term = lax.dot_general(
                left_ref[:, pl.ds(start, width)],
                right_ref[...],
                (((0,), (0,)), ((), ())),
                preferred_element_type=jnp.float32,
            )
            total = term if total is None else total + term
        gram_ref[upper * width : (upper + 1) * width, :] = total * inverse_total


def swap(block, bit):
    return lax.ppermute(block, bit, [(0, 1), (1, 0)])


def exclusive(block, place, axis):
    while block.shape[axis] > 1:
        half = block.shape[axis] // 2
        upper = lax.slice_in_dim(block, half, 2 * half, axis=axis)
        lower = lax.slice_in_dim(block, 0, half, axis=axis)
        block = jnp.where(place & half == half, upper, lower)
    return jnp.squeeze(block, axis)


def reduce_pairs(block, axes):
    own = lax.axis_index(axes)
    total = exclusive(block, own, 0)
    for flip in (3, 2, 1):
        route = [(i, i ^ flip) for i in range(4)]
        total += lax.ppermute(exclusive(block, own ^ flip, 0), axes, route)
    return total


def reduce_gram(block, high, low):
    first, rest = low[0], low[1:]
    block = block.reshape(2, -1, 2, *block.shape[2:])
    block = jnp.moveaxis(block, 2, 1).reshape(4, -1, *block.shape[3:])
    block = reduce_pairs(block, (high, first))
    while rest:
        if len(rest) >= 2:
            block = reduce_pairs(block.reshape(4, -1, *block.shape[1:]), (rest[-1], rest[-2]))
            rest = rest[:-2]
        else:
            last = rest[-1]
            own = lax.axis_index(last)
            block = block.reshape(2, -1, *block.shape[1:])
            block = exclusive(block, own, 0) + swap(exclusive(block, 1 - own, 0), last)
            rest = rest[:-1]
    return block[0]


def per_device(bits, design, signs, samples):
    rows, cols = design.shape
    samp = samples.shape[0]
    tiles = cols // LANES
    devices = 2 ** len(bits)
    high, core, low = bits[0], bits[1], bits[:1:-1]
    steps = [high, *low]
    own_index = lax.axis_index(tuple(bits))
    core_bit = len(low)

    own_sign = (2 * signs - 1).astype(jnp.float32).reshape(rows // BLOCK, BLOCK)
    oth_design = swap(design, core)
    oth_sign = swap(own_sign, core)
    listing = [steps[-1], *steps[:-1]]
    listed = lax.optimization_barrier(samples ^ (own_index >> len(bits)))
    listed = jnp.concatenate([listed, swap(samples, listing[0])])
    for i, bit in enumerate(listing[1:], 1):
        listed = jnp.concatenate([listed, swap(listed, bit)])
        if i == 1:
            own_blocks, zeros = transform_blocks(design, own_sign, listed.shape[0])
            listed = listed + zeros
        if i == len(steps) - 2:
            oth_blocks, zeros = transform_blocks(oth_design, oth_sign, listed.shape[0])
            listed = listed + zeros
    mixed = merge(own_blocks, oth_blocks)

    source = listed // rows
    parity = source & own_index
    shift = 1
    while shift < devices:
        parity = parity ^ (parity >> shift)
        shift *= 2
    at = ((source >> core_bit & 1) * rows + listed % rows) * tiles
    sign = (1 - 2 * (parity & 1)).astype(jnp.float32)

    third = samp // 6 * 2
    counts = [third + 0, third + 0]
    counts.append(samp - sum(counts))
    orders = []
    for part in range(3):
        order = [(part + i) % 3 for i in range(3)]
        orders.append(order + list(range(3, len(steps))))

    def plan(part, first):
        places = [listing.index(steps[bit]) for bit in orders[part]]
        return first << places[0], places[:0:-1], sum(counts[:part]), (samp, counts[part])

    parts = range(3)
    sent = gather([plan(part, 1) for part in parts], tiles, at, sign, mixed)
    arrived = [swap(sent[part], steps[part]) for part in parts]
    held = list(gather([plan(part, 0) for part in parts], tiles, at, sign, mixed))
    for level in range(1, 3):
        for part in parts:
            half = held[part].shape[0] // 2
            send = held[part][half:] + arrived[part][half:]
            held[part] = held[part][:half] + arrived[part][:half]
            arrived[part] = swap(send, steps[orders[part][level]])
    done = []
    for members in ((2,), (0,), (1,)):
        whole = jnp.concatenate(
            [(held[part] + arrived[part]).reshape(-1, counts[part] * tiles, LANES) for part in members], axis=1
        )
        for level in range(3, len(steps)):
            half = whole.shape[0] // 2
            whole = whole[:half] + swap(whole[half:], steps[level])
        done.append(whole[0])
    own_sum = jnp.concatenate([done[1], done[2], done[0]])
    oth_sum = swap(own_sum, core)

    half_rows = cols // 2
    sketch, product = pl.pallas_call(
        functools.partial(gram_kernel, 1.0 / math.sqrt(rows * devices), 1.0 / (samp * devices)),
        out_shape=[
            jax.ShapeDtypeStruct((samp, cols), jnp.float32),
            jax.ShapeDtypeStruct((half_rows, cols), jnp.float32),
        ],
        in_specs=[SMEM] + [VMEM] * 2,
        out_specs=[VMEM, VMEM],
        scratch_shapes=[pltpu.VMEM((2 * samp, cols), jnp.bfloat16)] * 2,
        compiler_params=limit(8),
        cost_estimate=cost(24 * samp * samp * cols, 16 * samp * cols),
    )(lax.axis_index(core).astype(jnp.int32).reshape(1), own_sum, oth_sum)

    gram = reduce_gram(product.reshape(2, 2 ** len(low), -1, cols), high, low)
    return sketch, gram


def solution(mesh):
    width = [size.bit_length() - 1 for size in mesh.devices.shape]
    bits = [f"{axis}{i}" for axis, w in zip(mesh.axis_names, width) for i in reversed(range(w))]
    split = Mesh(mesh.devices.reshape((2,) * len(bits)), tuple(bits))
    every = tuple(bits)
    return jax.shard_map(
        functools.partial(per_device, bits),
        mesh=split,
        in_specs=(P(every, None), P(every), P(every)),
        out_specs=(P(every, None), P(every, None)),
        check_vma=False,
    )
```
